32 devices in a mesh: dp: 4 (over z), context: 2 (over y), tensor: 4 (over x, core).
Axes of the slice: x: 2, y: 2, z: 4, core: 2. Of those that a mesh axis runs over, the one named last changes fastest.
Arguments:
- tokens: bfloat16 [4, 1024, 1024], P('dp', 'context'), may hold values from -6 to 6
- key_valid: int32 [4, 1024], P('dp', 'context'), may hold values from 0 to 1, as said below
- norm1_gain: bfloat16 [1024], P(('dp', 'context')), may hold values from 0.25 to 1.75
- norm1_shift: bfloat16 [1024], P(('dp', 'context')), may hold values from -4 to 4
- w_qkv: bfloat16 [1024, 3, 1024], P(('dp', 'context'), None, 'tensor'), may hold values from -0.25 to 0.25
- qv_bias: bfloat16 [2, 1024], P(None, ('tensor', 'dp', 'context')), may hold values from -4 to 4
- w_out: bfloat16 [1024, 1024], P('tensor', ('dp', 'context')), may hold values from -0.75 to 0.75
- out_bias: bfloat16 [1024], P(('dp', 'context')), may hold values from -4 to 4
- scale1: bfloat16 [1024], P(('dp', 'context')), may hold values from 0.5 to 1.5
- norm2_gain: bfloat16 [1024], P(('dp', 'context')), may hold values from 0.25 to 1.75
- norm2_shift: bfloat16 [1024], P(('dp', 'context')), may hold values from -4 to 4
- w_fc1: bfloat16 [1024, 4096], P(('dp', 'context'), 'tensor'), may hold values from -0.1875 to 0.1875
- fc1_bias: bfloat16 [4096], P(('tensor', 'dp', 'context')), may hold values from -4 to 4
- w_fc2: bfloat16 [4096, 1024], P('tensor', ('dp', 'context')), may hold values from -0.125 to 0.125
- fc2_bias: bfloat16 [1024], P(('dp', 'context')), may hold values from -4 to 4
- scale2: bfloat16 [1024], P(('dp', 'context')), may hold values from 0.5 to 1.5
- cotangent: bfloat16 [4, 1024, 1024], P('dp', 'context'), may hold values from -6 to 6
Outputs:
- block_out: bfloat16 [4, 1024, 1024], P('dp', 'context')
- token_grad: float32 [4, 1024, 1024], P('dp', 'context')
- norm1_gain_grad: float32 [1024], P(('dp', 'context'))
- norm1_shift_grad: float32 [1024], P(('dp', 'context'))
- w_qkv_grad: float32 [1024, 3, 1024], P(('dp', 'context'), None, 'tensor')
- qv_bias_grad: float32 [2, 1024], P(None, ('tensor', 'dp', 'context'))
- w_out_grad: float32 [1024, 1024], P('tensor', ('dp', 'context'))
- out_bias_grad: float32 [1024], P(('dp', 'context'))
- scale1_grad: float32 [1024], P(('dp', 'context'))
- norm2_gain_grad: float32 [1024], P(('dp', 'context'))
- norm2_shift_grad: float32 [1024], P(('dp', 'context'))
- w_fc1_grad: float32 [1024, 4096], P(('dp', 'context'), 'tensor')
- fc1_bias_grad: float32 [4096], P(('tensor', 'dp', 'context'))
- w_fc2_grad: float32 [4096, 1024], P('tensor', ('dp', 'context'))
- fc2_bias_grad: float32 [1024], P(('dp', 'context'))
- scale2_grad: float32 [1024], P(('dp', 'context'))
The draws below stay inside these ranges and needn't reach their ends.
Inputs may be any that keep to these rules, and one draw needn't show every extreme that they name: In each image the tokens with key_valid 1 come first; one or more padded tokens with key_valid 0 follow them.
All inputs are finite; a program needn't handle non-finite values.
Results may differ from the reference program's by a relative error of at most 0.02.
Values may be sent and summed in bfloat16 or wider, within the bound.
A program may use at most 128 MiB of HBM per device.

```python
import math
import jax
import jax.numpy as jnp
from jax import lax

D = 1024
HEADS = 16
HEAD_DIM = 64
FF = 4096
SEQ = 1024
IMAGES = 4


def draw_key_valid(key, part):
    key = jax.random.fold_in(key, 11)
    padded = jax.random.randint(key, (IMAGES,), 1, SEQ // 16 + 1)
    position = jnp.arange(SEQ)[None, :]
    return (position < (SEQ - padded)[:, None]).astype(jnp.int32)


def block_levels(stream_key, shape, split, smallest, largest):
    def one(dim, shards_of):
        steps = jax.random.uniform(jax.random.fold_in(jax.random.fold_in(stream_key, 6), dim), (shards_of,), jnp.float32, smallest / len(split), largest / len(split))
        return jnp.repeat(jnp.exp(steps), shape[dim] // shards_of).reshape((-1,) + (1,) * (len(shape) - dim - 1))

    level = one(*split[0])
    for cut in split[1:]:
        level = level * one(*cut)
    return level


def normal_values(rng, extent, scale, bound, pieces=(), kind=jnp.bfloat16):
    level = block_levels(rng, extent, pieces, -0.22, 0.18) if pieces else 1.0
    values = jax.random.normal(rng, extent, jnp.float32) * scale * level
    return jnp.minimum(jnp.maximum(values, -bound), bound).astype(kind)


def setup_inputs(seed: int = 0) -> dict:
    splits = jax.random.split(jax.random.key(seed), 18)
    tokens = normal_values(splits[0], (IMAGES, SEQ, D), 1.0, 6.0, ((0, 4), (1, 2)))
    key_valid = draw_key_valid(jax.random.fold_in(splits[17], 71), 0)
    norm1_gain = jnp.clip(1.0 + 0.15 * jax.random.normal(splits[2], (D,), jnp.float32), 0.25, 1.75).astype(jnp.bfloat16)
    norm1_shift = normal_values(splits[3], (D,), 0.3, 4.0, ((0, 8),))
    w_qkv = normal_values(splits[4], (D, 3, D), (D // 2) ** -0.5, 0.25, ((0, 8), (2, 4)))
    qv_bias = normal_values(splits[5], (2, D), 0.5, 4.0, ((1, 32),))
    w_out = normal_values(splits[6], (D, D), (D // 16) ** -0.5, 0.75, ((0, 4), (1, 8)))
    out_bias = normal_values(splits[7], (D,), 0.3, 4.0, ((0, 8),))
    scale1 = jnp.clip(0.5 + 1.0 * jax.random.uniform(splits[8], (D,), jnp.float32) ** block_levels(splits[8], (D,), ((0, 8),), -0.2, 0.2), 0.5, 1.5).astype(jnp.bfloat16)
    norm2_gain = jnp.clip(1.0 + 0.15 * jax.random.normal(splits[9], (D,), jnp.float32), 0.25, 1.75).astype(jnp.bfloat16)
    norm2_shift = normal_values(splits[10], (D,), 0.3, 4.0, ((0, 8),))
    w_fc1 = normal_values(splits[11], (D, FF), D ** -0.5, 0.1875, ((0, 8), (1, 4)))
    fc1_bias = normal_values(splits[12], (FF,), 0.5, 4.0, ((0, 32),))
    w_fc2 = normal_values(splits[13], (FF, D), (FF // 2) ** -0.5, 0.125, ((0, 4), (1, 8)))
    fc2_bias = normal_values(splits[14], (D,), 0.3, 4.0, ((0, 8),))
    scale2 = jnp.clip(0.5 + 1.0 * jax.random.uniform(splits[15], (D,), jnp.float32) ** block_levels(splits[15], (D,), ((0, 8),), -0.2, 0.2), 0.5, 1.5).astype(jnp.bfloat16)
    cotangent = normal_values(splits[16], (IMAGES, SEQ, D), 1.0, 6.0, ((0, 4), (1, 2)))
    return {"tokens": tokens, "key_valid": key_valid, "norm1_gain": norm1_gain, "norm1_shift": norm1_shift, "w_qkv": w_qkv, "qv_bias": qv_bias, "w_out": w_out, "out_bias": out_bias, "scale1": scale1, "norm2_gain": norm2_gain, "norm2_shift": norm2_shift, "w_fc1": w_fc1, "fc1_bias": fc1_bias, "w_fc2": w_fc2, "fc2_bias": fc2_bias, "scale2": scale2, "cotangent": cotangent}


@jax.custom_vjp
def low(v):
    return lax.optimization_barrier(v.astype(jnp.bfloat16)).astype(jnp.float32)

@jax.custom_vjp
def low_back(v):
    return v

def low_keep(v):
    return (low(v), None)

def low_pass(kept, grad):
    return (grad,)

def back_keep(v):
    return (v, None)

def back_low(kept, grad):
    return (low(grad),)
low.defvjp(low_keep, low_pass)
low_back.defvjp(back_keep, back_low)
EPSILON = 1e-06
NEGATIVE = -1e+30
PRECISE = lax.Precision.HIGHEST

def rounded_both(value):
    return low_back(low(value))

def layer_norm(value, gain, shift):
    average = lax.optimization_barrier(jnp.mean(value, axis=-1, keepdims=True))
    centred = value - average
    variance = lax.optimization_barrier(jnp.mean(centred * centred, axis=-1, keepdims=True))
    return centred * lax.rsqrt(variance + EPSILON) * gain + shift

def forward(params, residual, key_mask):
    gain_one, shift_one, w_qkv, qv_bias, w_out, out_bias, scale1, gain_two, shift_two, w_fc1, fc1_bias, w_fc2, fc2_bias, scale2 = params
    normed_one = low(layer_norm(residual, gain_one, shift_one))
    queries = rounded_both(jnp.dot(normed_one, w_qkv[:, 0], precision=PRECISE) + qv_bias[0])
    key_rows = rounded_both(jnp.dot(normed_one, w_qkv[:, 1], precision=PRECISE))
    values = rounded_both(jnp.dot(normed_one, w_qkv[:, 2], precision=PRECISE) + qv_bias[1])
    key_heads = key_rows.reshape(SEQ, HEADS, HEAD_DIM)
    value_heads = values.reshape(SEQ, HEADS, HEAD_DIM)
    allowed = (key_mask > 0)[None, None, :]
    block_rows = math.gcd(SEQ, 512)

    def attend_block(query_block):
        scores = jnp.einsum('bhe,nhe->hbn', query_block, key_heads, precision=PRECISE) * HEAD_DIM ** (-0.5)
        scores = low_back(jnp.where(allowed, scores, NEGATIVE))
        highest = lax.optimization_barrier(jnp.max(scores, axis=-1, keepdims=True))
        expo = jnp.exp(scores - highest)
        probs = expo / lax.optimization_barrier(jnp.sum(expo, axis=-1, keepdims=True))
        return jnp.einsum('hbn,nhe->bhe', low(probs), value_heads, precision=PRECISE)
    blocks = lax.map(jax.checkpoint(attend_block), queries.reshape(SEQ // block_rows, block_rows, HEADS, HEAD_DIM))
    attended = rounded_both(blocks.reshape(SEQ, HEADS * HEAD_DIM))
    branch = low_back(jnp.dot(attended, w_out, precision=PRECISE) + out_bias)
    residual_one = residual + scale1 * branch
    normed_two = low(layer_norm(residual_one, gain_two, shift_two))
    pre_act = low_back(jnp.dot(normed_two, w_fc1, precision=PRECISE) + fc1_bias)
    hidden = low(jax.nn.gelu(pre_act, approximate=False))
    mlp_out = low_back(jnp.dot(hidden, w_fc2, precision=PRECISE) + fc2_bias)
    return residual_one + scale2 * mlp_out

def reference(tokens, key_valid, norm1_gain, norm1_shift, w_qkv, qv_bias, w_out, out_bias, scale1, norm2_gain, norm2_shift, w_fc1, fc1_bias, w_fc2, fc2_bias, scale2, cotangent):
    params = tuple((array.astype(jnp.float32) for array in (norm1_gain, norm1_shift, w_qkv, qv_bias, w_out, out_bias, scale1, norm2_gain, norm2_shift, w_fc1, fc1_bias, w_fc2, fc2_bias, scale2)))

    def one_image(totals, entry):
        image, mask_row, cot_rows = entry
        output, pull = jax.vjp(lambda weights, rows_in: forward(weights, rows_in, mask_row), params, image.astype(jnp.float32))
        grad_params, grad_rows = pull(cot_rows.astype(jnp.float32))
        totals = jax.tree.map(lambda summed, adding: summed + adding, totals, grad_params)
        return (totals, (output.astype(jnp.bfloat16), grad_rows))
    initial = jax.tree.map(jnp.zeros_like, params)
    totals, (outputs, token_grads) = lax.scan(one_image, initial, (tokens, key_valid, cotangent))
    grad_gain_one, grad_shift_one, grad_qkv, grad_qv, grad_wout, grad_bout, grad_scale_one, grad_gain_two, grad_shift_two, grad_fc1, grad_bfc1, grad_fc2, grad_bfc2, grad_scale_two = totals
    return (outputs, token_grads, grad_gain_one, grad_shift_one, grad_qkv, grad_qv, grad_wout, grad_bout, grad_scale_one, grad_gain_two, grad_shift_two, grad_fc1, grad_bfc1, grad_fc2, grad_bfc2, grad_scale_two)
```

```python
import functools
import math

import jax
import jax.numpy as jnp
from jax import lax
from jax.experimental import pallas as pl
from jax.experimental.pallas import tpu as pltpu
from jax.sharding import PartitionSpec as P

HEAD_DIM = 64
MESH = pl.DeviceIdType.MESH
VMEM_LIMIT = 56 * 1024 * 1024

EPSILON = 1e-06
NEGATIVE = -1e30


def normalize(value):
    average = jnp.mean(value, axis=-1, keepdims=True)
    centred = value - average
    inv_std = lax.rsqrt(jnp.mean(centred * centred, axis=-1, keepdims=True) + EPSILON)
    return (centred * inv_std, inv_std)


def norm_backward(grad_norm, normed, inv_std, gain):
    scaled = grad_norm * gain
    return (
        scaled
        - jnp.mean(scaled, axis=-1, keepdims=True)
        - normed * jnp.mean(scaled * normed, axis=-1, keepdims=True)
    ) * inv_std


def contract_rows(first_matrix, second_matrix):
    return lax.dot_general(
        first_matrix, second_matrix, (((0,), (0,)), ((), ())), preferred_element_type=jnp.float32
    )


def contract_cols(first_matrix, second_matrix):
    return lax.dot_general(
        first_matrix, second_matrix, (((1,), (1,)), ((), ())), preferred_element_type=jnp.float32
    )


def attend(carry, query_heads, key_rows, value_rows, key_mask):
    running_max, running_total, running_sum = carry
    key_count = key_rows.shape[0]
    head_count = query_heads.shape[1]
    for offset in range(0, key_count, 512):
        finish = min(key_count, offset + 512)
        key_block = key_rows[offset:finish].reshape(finish - offset, head_count, HEAD_DIM)
        value_block = value_rows[offset:finish].reshape(finish - offset, head_count, HEAD_DIM)
        mask_block = key_mask[offset:finish][None, None, :] > 0
        scores = jnp.einsum(
            "rhe,nhe->rhn", query_heads, key_block, preferred_element_type=jnp.float32
        ) * HEAD_DIM ** (-0.5)
        scores = jnp.where(mask_block, scores, NEGATIVE)
        new_max = jnp.maximum(running_max, jnp.max(scores, axis=-1, keepdims=True))
        weights = jnp.where(mask_block, jnp.exp(scores - new_max), 0.0)
        factor = jnp.exp(running_max - new_max)
        running_total = running_total * factor + jnp.sum(weights, axis=-1, keepdims=True)
        running_sum = running_sum * factor + jnp.einsum(
            "rhn,nhe->rhe",
            weights.astype(jnp.bfloat16),
            value_block,
            preferred_element_type=jnp.float32,
        )
        running_max = new_max
    return (running_max, running_total, running_sum)


def params(ident):
    return pltpu.CompilerParams(
        collective_id=ident, has_side_effects=True, vmem_limit_bytes=VMEM_LIMIT
    )


def greet(count, device_id):
    pl.semaphore_signal(
        pltpu.get_barrier_semaphore(), inc=count, device_id=device_id, device_id_type=MESH
    )


def remote(src, dst, send_sem, recv_sem, device_id):
    return pltpu.make_async_remote_copy(
        src_ref=src,
        dst_ref=dst,
        send_sem=send_sem,
        recv_sem=recv_sem,
        device_id=device_id,
        device_id_type=MESH,
    )


def greet_line(line):
    here = lax.axis_index("dp")
    side = lax.axis_index("context")
    greet(1, {"context": 1 - side})

    @pl.when(here < line - 1)
    def _():
        greet(1, {"dp": here + 1})

    @pl.when(here > 0)
    def _():
        greet(1, {"dp": here - 1})

    above = jnp.where(here < line - 1, 1, 0)
    below = jnp.where(here > 0, 1, 0)
    pl.semaphore_wait(pltpu.get_barrier_semaphore(), 1 + above + below)


def owner_view(ref, owner, width):
    if len(ref.shape) == 3:
        return ref.at[owner]
    return ref.at[:, pl.ds(pl.multiple_of(owner * width, width), width)]


def gather_kernel(line, count, *refs):
    ins, outs = refs[:count], refs[count : 2 * count]
    send, recv, local = refs[2 * count :]
    here = lax.axis_index("dp")
    side = lax.axis_index("context")
    cross = 2 * (line - 1)

    def part(a, row, column):
        return owner_view(outs[a], row * 2 + column, ins[a].shape[-1])

    def up(a, s, row):
        src = ins[a] if s == 0 else part(a, row, side)
        return remote(
            src, part(a, row, side), send.at[a, s], recv.at[a, s], {"dp": here + 1}
        )

    def down(a, s, row):
        src = ins[a] if s == 0 else part(a, row, side)
        slot = line - 1 + s
        return remote(
            src, part(a, row, side), send.at[a, slot], recv.at[a, slot], {"dp": here - 1}
        )

    def over(a, row, own):
        src = ins[a] if own else part(a, row, side)
        return remote(
            src,
            part(a, row, side),
            send.at[a, cross + row],
            recv.at[a, cross + row],
            {"context": 1 - side},
        )

    greet_line(line)
    for a in range(count):

        @pl.when(here < line - 1)
        def _():
            up(a, 0, here).start()

        @pl.when(here > 0)
        def _():
            down(a, 0, here).start()

        over(a, here, True).start()
        pltpu.make_async_copy(ins[a], part(a, here, side), local.at[a]).start()
    for s in range(1, line):
        for a in range(count):

            @pl.when(here - s >= 0)
            def _():
                up(a, s - 1, here - s).wait_recv()

                @pl.when(here < line - 1)
                def _():
                    up(a, s, here - s).start()

                over(a, here - s, False).start()

            @pl.when(here + s <= line - 1)
            def _():
                down(a, s - 1, here + s).wait_recv()

                @pl.when(here > 0)
                def _():
                    down(a, s, here + s).start()

                over(a, here + s, False).start()

    for a in range(count):
        pltpu.make_async_copy(ins[a], part(a, here, side), local.at[a]).wait()
        for row in range(line):
            remote(
                part(a, row, 1 - side),
                part(a, row, 1 - side),
                send.at[a, cross + row],
                recv.at[a, cross + row],
                {"context": 1 - side},
            ).wait_recv()
            over(a, row, False).wait_send()
        for s in range(line - 1):

            @pl.when((here < line - 1) & (here - s >= 0))
            def _():
                up(a, s, here - s).wait_send()

            @pl.when((here > 0) & (here + s <= line - 1))
            def _():
                down(a, s, here + s).wait_send()


def gather_parts(arrays, stacked, line, ident):
    owners = line * 2
    shapes = []
    for array, stack in zip(arrays, stacked):
        if stack:
            shape = (owners,) + array.shape
        else:
            shape = (array.shape[0], owners * array.shape[1])
        shapes.append(jax.ShapeDtypeStruct(shape, array.dtype))
    count = len(arrays)
    slots = 2 * (line - 1) + line
    return pl.pallas_call(
        functools.partial(gather_kernel, line, count),
        out_shape=tuple(shapes),
        in_specs=[pl.BlockSpec(memory_space=pl.ANY)] * count,
        out_specs=tuple([pl.BlockSpec(memory_space=pl.ANY)] * count),
        scratch_shapes=[
            pltpu.SemaphoreType.DMA((count, slots)),
            pltpu.SemaphoreType.DMA((count, slots)),
            pltpu.SemaphoreType.DMA((count,)),
        ],
        compiler_params=params(ident),
    )(*arrays)


def swap_kernel(in_ref, out_ref, send, recv):
    side = lax.axis_index("context")
    greet(1, {"context": 1 - side})
    pl.semaphore_wait(pltpu.get_barrier_semaphore(), 1)
    copy = remote(in_ref, out_ref, send, recv, {"context": 1 - side})
    copy.start()
    copy.wait()


def swap(array, ident):
    return pl.pallas_call(
        swap_kernel,
        out_shape=jax.ShapeDtypeStruct(array.shape, array.dtype),
        in_specs=[pl.BlockSpec(memory_space=pl.ANY)],
        out_specs=pl.BlockSpec(memory_space=pl.ANY),
        scratch_shapes=[pltpu.SemaphoreType.DMA, pltpu.SemaphoreType.DMA],
        compiler_params=params(ident),
    )(array)


PIECES = 4


def tensor_sum_kernel(count, *refs):
    ins, outs = refs[:count], refs[count : 2 * count]
    pair_buf, sum_buf, far_buf, send, recv = refs[2 * count :]
    place = lax.axis_index("tensor")
    core = lax.rem(place, 2)
    pair = {"tensor": place + 1 - 2 * core}
    far = {"tensor": lax.rem(place + 2, 4)}
    greet(1, pair)
    greet(1, far)
    pl.semaphore_wait(pltpu.get_barrier_semaphore(), 2)
    half = ins[0].shape[0] // 2
    step = half // PIECES

    def rows(which, p):
        return pl.ds(pl.multiple_of(which * half + p * step, step), step)

    def first(a, p):
        return remote(
            ins[a].at[rows(1 - core, p)],
            pair_buf.at[a, p],
            send.at[0, a, p],
            recv.at[0, a, p],
            pair,
        )

    def second(a, p):
        return remote(
            sum_buf.at[a, p], far_buf.at[a, p], send.at[1, a, p], recv.at[1, a, p], far
        )

    def third(a, p):
        return remote(
            outs[a].at[rows(core, p)],
            outs[a].at[rows(core, p)],
            send.at[2, a, p],
            recv.at[2, a, p],
            pair,
        )

    todo = [(a, p) for a in range(count) for p in range(PIECES)]
    for a, p in todo:
        first(a, p).start()
    for a, p in todo:
        first(a, p).wait_recv()
        total = ins[a][rows(core, p), :].astype(jnp.float32) + pair_buf[a, p].astype(jnp.float32)
        sum_buf[a, p] = total.astype(jnp.bfloat16)
        second(a, p).start()
    for a, p in todo:
        second(a, p).wait_recv()
        total = sum_buf[a, p].astype(jnp.float32) + far_buf[a, p].astype(jnp.float32)
        outs[a][rows(core, p), :] = total.astype(jnp.bfloat16)
        third(a, p).start()
    for a, p in todo:
        remote(
            outs[a].at[rows(1 - core, p)],
            outs[a].at[rows(1 - core, p)],
            send.at[2, a, p],
            recv.at[2, a, p],
            pair,
        ).wait_recv()
        first(a, p).wait_send()
        second(a, p).wait_send()
        third(a, p).wait_send()


def tensor_sum(arrays, ident):
    count = len(arrays)
    rows, width = arrays[0].shape
    buf = pltpu.VMEM((count, PIECES, rows // 2 // PIECES, width), jnp.bfloat16)
    return pl.pallas_call(
        functools.partial(tensor_sum_kernel, count),
        out_shape=tuple(jax.ShapeDtypeStruct(a.shape, a.dtype) for a in arrays),
        in_specs=[pl.BlockSpec(memory_space=pltpu.VMEM)] * count,
        out_specs=tuple([pl.BlockSpec(memory_space=pltpu.VMEM)] * count),
        scratch_shapes=[
            buf,
            buf,
            buf,
            pltpu.SemaphoreType.DMA((3, count, PIECES)),
            pltpu.SemaphoreType.DMA((3, count, PIECES)),
        ],
        compiler_params=params(ident),
    )(*arrays)


def add_rows(dst, terms):
    count, width = dst.shape
    block = math.gcd(count, 64 if width > 512 else 256)

    def body(i, carry):
        at = pl.ds(pl.multiple_of(i * block, block), block)
        total = terms[0][at, :].astype(jnp.float32)
        for term in terms[1:]:
            total = total + term[at, :].astype(jnp.float32)
        dst[at, :] = total.astype(dst.dtype)
        return carry

    lax.fori_loop(0, count // block, body, 0)


def scatter_kernel(line, count, *refs):
    ins, outs = refs[:count], refs[count : 2 * count]
    cross = refs[2 * count : 3 * count]
    climb = refs[3 * count : 4 * count]
    fall = refs[4 * count : 5 * count]
    send, recv = refs[5 * count :]
    here = lax.axis_index("dp")
    side = lax.axis_index("context")

    def mine(a, row, column):
        return owner_view(ins[a], row * 2 + column, outs[a].shape[-1])

    def over(a, row):
        return remote(
            mine(a, row, 1 - side),
            cross[a].at[row],
            send.at[0, a, row],
            recv.at[0, a, row],
            {"context": 1 - side},
        )

    def up(a, row):
        return remote(
            cross[a].at[row],
            climb[a].at[row],
            send.at[1, a, row],
            recv.at[1, a, row],
            {"dp": here + 1},
        )

    def down(a, row):
        return remote(
            cross[a].at[row],
            fall[a].at[row],
            send.at[2, a, row],
            recv.at[2, a, row],
            {"dp": here - 1},
        )

    greet_line(line)
    for k in range(line // 2):
        for a in range(count):
            over(a, line - 1 - k).start()
            over(a, k).start()
    for k in range(line - 1):
        for a in range(count):
            high, low = line - 1 - k, k

            @pl.when(here < high)
            def _():
                over(a, high).wait_recv()

                @pl.when(here == 0)
                def _():
                    add_rows(cross[a].at[high], [mine(a, high, side), cross[a].at[high]])

                @pl.when(here > 0)
                def _():
                    up(a, high).wait_recv()
                    add_rows(
                        cross[a].at[high],
                        [mine(a, high, side), cross[a].at[high], climb[a].at[high]],
                    )

                up(a, high).start()

            @pl.when(here > low)
            def _():
                over(a, low).wait_recv()

                @pl.when(here == line - 1)
                def _():
                    add_rows(cross[a].at[low], [mine(a, low, side), cross[a].at[low]])

                @pl.when(here < line - 1)
                def _():
                    down(a, low).wait_recv()
                    add_rows(
                        cross[a].at[low],
                        [mine(a, low, side), cross[a].at[low], fall[a].at[low]],
                    )

                down(a, low).start()

    for a in range(count):
        over(a, here).wait_recv()
        own = [mine(a, here, side), cross[a].at[here]]

        @pl.when(here == 0)
        def _():
            down(a, here).wait_recv()
            add_rows(outs[a], own + [fall[a].at[here]])

        @pl.when(here == line - 1)
        def _():
            up(a, here).wait_recv()
            add_rows(outs[a], own + [climb[a].at[here]])

        @pl.when((here > 0) & (here < line - 1))
        def _():
            down(a, here).wait_recv()
            up(a, here).wait_recv()
            add_rows(outs[a], own + [climb[a].at[here], fall[a].at[here]])

    for a in range(count):
        for row in range(line):
            over(a, row).wait_send()

            @pl.when(here < row)
            def _():
                up(a, row).wait_send()

            @pl.when(here > row)
            def _():
                down(a, row).wait_send()


def scatter_parts(arrays, line, ident):
    owners = 2 * line
    count = len(arrays)
    outs = []
    for array in arrays:
        if array.ndim == 3:
            outs.append(array.shape[1:])
        else:
            outs.append((array.shape[0], array.shape[1] // owners))
    bufs = [pltpu.VMEM((line,) + o, a.dtype) for o, a in zip(outs, arrays)]
    return pl.pallas_call(
        functools.partial(scatter_kernel, line, count),
        out_shape=tuple(jax.ShapeDtypeStruct(o, jnp.float32) for o in outs),
        in_specs=[pl.BlockSpec(memory_space=pltpu.VMEM)] * count,
        out_specs=tuple([pl.BlockSpec(memory_space=pltpu.VMEM)] * count),
        scratch_shapes=bufs * 3
        + [pltpu.SemaphoreType.DMA((3, count, line)), pltpu.SemaphoreType.DMA((3, count, line))],
        compiler_params=params(ident),
    )(*arrays)


def pack_rows(vectors, owners, dtype):
    rows = [v.reshape(owners, -1).astype(dtype) for v in vectors]
    rows = [jnp.pad(r, ((0, 0), (0, -r.shape[1] % 128))).reshape(owners, -1, 128) for r in rows]
    packed = jnp.concatenate(rows, axis=1)
    return jnp.pad(packed, ((0, 0), (0, 16 - packed.shape[1]), (0, 0)))

def on_device(
    tokens,
    key_valid,
    norm1_gain,
    norm1_shift,
    w_qkv,
    qv_bias,
    w_out,
    out_bias,
    scale1,
    norm2_gain,
    norm2_shift,
    w_fc1,
    fc1_bias,
    w_fc2,
    fc2_bias,
    scale2,
    cotangent,
):
    gathered = (
        lax.all_gather(norm1_gain, ("dp", "context"), axis=0, tiled=True),
        lax.all_gather(norm1_shift, ("dp", "context"), axis=0, tiled=True),
        lax.all_gather(w_qkv, ("dp", "context"), axis=0, tiled=True),
        lax.all_gather(qv_bias, ("dp", "context"), axis=1, tiled=True),
        lax.all_gather(w_out, ("dp", "context"), axis=1, tiled=True),
        lax.all_gather(out_bias, ("dp", "context"), axis=0, tiled=True),
        lax.all_gather(scale1, ("dp", "context"), axis=0, tiled=True),
        lax.all_gather(norm2_gain, ("dp", "context"), axis=0, tiled=True),
        lax.all_gather(norm2_shift, ("dp", "context"), axis=0, tiled=True),
        lax.all_gather(w_fc1, ("dp", "context"), axis=0, tiled=True),
        lax.all_gather(fc1_bias, ("dp", "context"), axis=0, tiled=True),
        lax.all_gather(w_fc2, ("dp", "context"), axis=1, tiled=True),
        lax.all_gather(fc2_bias, ("dp", "context"), axis=0, tiled=True),
        lax.all_gather(scale2, ("dp", "context"), axis=0, tiled=True),
    )
    (
        gain_one,
        shift_one,
        qkv_full,
        qv_full,
        out_full,
        bias_out,
        scale_one,
        gain_two,
        shift_two,
        fc1_full,
        bias_fc1,
        fc2_full,
        bias_fc2,
        scale_two,
    ) = gathered
    gain_one = gain_one.astype(jnp.float32)
    shift_one = shift_one.astype(jnp.float32)
    bias_out = bias_out.astype(jnp.float32)
    scale_one = scale_one.astype(jnp.float32)
    gain_two = gain_two.astype(jnp.float32)
    shift_two = shift_two.astype(jnp.float32)
    bias_fc1 = bias_fc1.astype(jnp.float32)
    bias_fc2 = bias_fc2.astype(jnp.float32)
    scale_two = scale_two.astype(jnp.float32)
    qv_float = qv_full.astype(jnp.float32)
    residual = tokens[0].astype(jnp.float32)
    row_count = residual.shape[0]
    model_width = residual.shape[1]
    local_width = qkv_full.shape[2]
    head_count = local_width // HEAD_DIM
    normed_one, inv_one = normalize(residual)
    hidden_one = (normed_one * gain_one + shift_one).astype(jnp.bfloat16)
    projected = jnp.dot(
        hidden_one,
        qkv_full.reshape(model_width, 3 * local_width),
        preferred_element_type=jnp.float32,
    ).reshape(row_count, 3, local_width)
    queries = (projected[:, 0] + qv_float[0]).astype(jnp.bfloat16)
    key_rows = projected[:, 1].astype(jnp.bfloat16)
    values = (projected[:, 2] + qv_float[1]).astype(jnp.bfloat16)
    query_heads = queries.reshape(row_count, head_count, HEAD_DIM)
    key_mask = key_valid[0].astype(jnp.bfloat16)
    start_carry = (
        jnp.full((row_count, head_count, 1), NEGATIVE, jnp.float32),
        jnp.zeros((row_count, head_count, 1), jnp.float32),
        jnp.zeros((row_count, head_count, HEAD_DIM), jnp.float32),
    )
    running_max, running_total, running_sum = attend(
        start_carry,
        query_heads,
        lax.all_gather(key_rows, "context", axis=0, tiled=True),
        lax.all_gather(values, "context", axis=0, tiled=True),
        lax.all_gather(key_mask, "context", axis=0, tiled=True),
    )
    attn_heads = running_sum / running_total
    log_total = running_max + jnp.log(running_total)
    attended = attn_heads.reshape(row_count, local_width).astype(jnp.bfloat16)
    branch = (
        lax.psum(
            jnp.dot(attended, out_full, preferred_element_type=jnp.float32).astype(jnp.bfloat16),
            "tensor",
        ).astype(jnp.float32)
        + bias_out
    )
    residual_one = residual + scale_one * branch
    normed_two, inv_two = normalize(residual_one)
    hidden_two = (normed_two * gain_two + shift_two).astype(jnp.bfloat16)
    pre_act = jnp.dot(hidden_two, fc1_full, preferred_element_type=jnp.float32) + bias_fc1
    activated, gelu_pull = jax.vjp(lambda value: jax.nn.gelu(value, approximate=False), pre_act)
    hidden = activated.astype(jnp.bfloat16)
    mlp_out = (
        lax.psum(
            jnp.dot(hidden, fc2_full, preferred_element_type=jnp.float32).astype(jnp.bfloat16),
            "tensor",
        ).astype(jnp.float32)
        + bias_fc2
    )
    block_out = (residual_one + scale_two * mlp_out).astype(jnp.bfloat16)
    back_weights = (
        lax.all_gather(w_qkv, ("dp", "context"), axis=0, tiled=True),
        lax.all_gather(w_out, ("dp", "context"), axis=1, tiled=True),
        lax.all_gather(w_fc1, ("dp", "context"), axis=0, tiled=True),
        lax.all_gather(w_fc2, ("dp", "context"), axis=1, tiled=True),
    )
    qkv_back, out_back, fc1_back, fc2_back = back_weights
    grad_out = cotangent[0].astype(jnp.float32)
    grad_scale_two = jnp.sum(grad_out * mlp_out, axis=0)
    grad_mlp = (grad_out * scale_two).astype(jnp.bfloat16)
    grad_bias_fc2 = jnp.sum(grad_mlp.astype(jnp.float32), axis=0)
    grad_fc2 = contract_rows(hidden, grad_mlp)
    grad_act = contract_cols(grad_mlp, fc2_back)
    grad_pre = gelu_pull(grad_act)[0].astype(jnp.bfloat16)
    grad_bias_fc1 = jnp.sum(grad_pre.astype(jnp.float32), axis=0)
    grad_fc1 = contract_rows(hidden_two, grad_pre)
    grad_hidden_two = lax.psum(
        contract_cols(grad_pre, fc1_back).astype(jnp.bfloat16), "tensor"
    ).astype(jnp.float32)
    grad_gain_two = jnp.sum(grad_hidden_two * normed_two, axis=0)
    grad_shift_two = jnp.sum(grad_hidden_two, axis=0)
    grad_residual_one = grad_out + norm_backward(grad_hidden_two, normed_two, inv_two, gain_two)
    grad_scale_one = jnp.sum(grad_residual_one * branch, axis=0)
    grad_branch = (grad_residual_one * scale_one).astype(jnp.bfloat16)
    grad_bias_out = jnp.sum(grad_branch.astype(jnp.float32), axis=0)
    grad_wout = contract_rows(attended, grad_branch)
    grad_attended = contract_cols(grad_branch, out_back).astype(jnp.bfloat16)
    grad_attn_heads = grad_attended.reshape(row_count, head_count, HEAD_DIM)
    row_delta = jnp.sum(grad_attn_heads.astype(jnp.float32) * attn_heads, axis=-1, keepdims=True)
    back_keys, back_values, back_mask = (
        lax.all_gather(key_rows, "context", axis=0, tiled=True),
        lax.all_gather(values, "context", axis=0, tiled=True),
        lax.all_gather(key_mask, "context", axis=0, tiled=True),
    )
    key_count = back_keys.shape[0]
    grad_query = jnp.zeros((row_count, head_count, HEAD_DIM), jnp.float32)
    key_terms = []
    value_terms = []
    for offset in range(0, key_count, 512):
        finish = min(key_count, offset + 512)
        key_block = back_keys[offset:finish].reshape(finish - offset, head_count, HEAD_DIM)
        value_block = back_values[offset:finish].reshape(finish - offset, head_count, HEAD_DIM)
        mask_block = back_mask[offset:finish][None, None, :] > 0
        scores = jnp.einsum(
            "rhe,nhe->rhn", query_heads, key_block, preferred_element_type=jnp.float32
        ) * HEAD_DIM ** (-0.5)
        attn_prob = jnp.where(mask_block, jnp.exp(scores - log_total), 0.0)
        value_terms.append(
            jnp.einsum(
                "rhn,rhe->nhe",
                attn_prob.astype(jnp.bfloat16),
                grad_attn_heads,
                preferred_element_type=jnp.float32,
            )
        )
        grad_prob = jnp.einsum(
            "rhe,nhe->rhn", grad_attn_heads, value_block, preferred_element_type=jnp.float32
        )
        grad_scores = (attn_prob * (grad_prob - row_delta)).astype(jnp.bfloat16)
        grad_query = grad_query + jnp.einsum(
            "rhn,nhe->rhe", grad_scores, key_block, preferred_element_type=jnp.float32
        ) * HEAD_DIM ** (-0.5)
        key_terms.append(
            jnp.einsum("rhn,rhe->nhe", grad_scores, query_heads, preferred_element_type=jnp.float32)
            * HEAD_DIM ** (-0.5)
        )
    key_sums = jnp.concatenate(key_terms, axis=0).reshape(key_count, local_width)
    value_sums = jnp.concatenate(value_terms, axis=0).reshape(key_count, local_width)
    grad_keys, grad_values = (
        lax.psum_scatter(
            key_sums.astype(jnp.bfloat16), "context", scatter_dimension=0, tiled=True
        ).astype(jnp.float32),
        lax.psum_scatter(
            value_sums.astype(jnp.bfloat16), "context", scatter_dimension=0, tiled=True
        ).astype(jnp.float32),
    )
    grad_projected = jnp.stack(
        [grad_query.reshape(row_count, local_width), grad_keys, grad_values], axis=1
    ).astype(jnp.bfloat16)
    grad_float = grad_projected.astype(jnp.float32)
    grad_qv = jnp.stack(
        [jnp.sum(grad_float[:, 0], axis=0), jnp.sum(grad_float[:, 2], axis=0)], axis=0
    )
    grad_flat = grad_projected.reshape(row_count, 3 * local_width)
    grad_qkv = contract_rows(hidden_one, grad_flat).reshape(model_width, 3, local_width)
    grad_hidden_one = lax.psum(
        contract_cols(grad_flat, qkv_back.reshape(model_width, 3 * local_width)).astype(
            jnp.bfloat16
        ),
        "tensor",
    ).astype(jnp.float32)
    grad_gain_one = jnp.sum(grad_hidden_one * normed_one, axis=0)
    grad_shift_one = jnp.sum(grad_hidden_one, axis=0)
    token_grad = grad_residual_one + norm_backward(grad_hidden_one, normed_one, inv_one, gain_one)
    shards = (
        lax.psum_scatter(grad_gain_one, ("dp", "context"), scatter_dimension=0, tiled=True),
        lax.psum_scatter(grad_shift_one, ("dp", "context"), scatter_dimension=0, tiled=True),
        lax.psum_scatter(grad_qkv, ("dp", "context"), scatter_dimension=0, tiled=True),
        lax.psum_scatter(grad_qv, ("dp", "context"), scatter_dimension=1, tiled=True),
        lax.psum_scatter(grad_wout, ("dp", "context"), scatter_dimension=1, tiled=True),
        lax.psum_scatter(grad_bias_out, ("dp", "context"), scatter_dimension=0, tiled=True),
        lax.psum_scatter(grad_scale_one, ("dp", "context"), scatter_dimension=0, tiled=True),
        lax.psum_scatter(grad_gain_two, ("dp", "context"), scatter_dimension=0, tiled=True),
        lax.psum_scatter(grad_shift_two, ("dp", "context"), scatter_dimension=0, tiled=True),
        lax.psum_scatter(grad_fc1, ("dp", "context"), scatter_dimension=0, tiled=True),
        lax.psum_scatter(grad_bias_fc1, ("dp", "context"), scatter_dimension=0, tiled=True),
        lax.psum_scatter(grad_fc2, ("dp", "context"), scatter_dimension=1, tiled=True),
        lax.psum_scatter(grad_bias_fc2, ("dp", "context"), scatter_dimension=0, tiled=True),
        lax.psum_scatter(grad_scale_two, ("dp", "context"), scatter_dimension=0, tiled=True),
    )
    return (block_out[None], token_grad[None]) + tuple(shards)


def on_device_line(
    line,
    tokens,
    key_valid,
    norm1_gain,
    norm1_shift,
    w_qkv,
    qv_bias,
    w_out,
    out_bias,
    scale1,
    norm2_gain,
    norm2_shift,
    w_fc1,
    fc1_bias,
    w_fc2,
    fc2_bias,
    scale2,
    cotangent,
):
    owners = 2 * line
    mask_row = key_valid[0].astype(jnp.bfloat16)
    packed = pack_rows(
        [
            norm1_gain,
            norm1_shift,
            out_bias,
            scale1,
            norm2_gain,
            norm2_shift,
            fc2_bias,
            scale2,
            fc1_bias,
            qv_bias,
            mask_row,
        ],
        1,
        jnp.bfloat16,
    )[0]
    pack_full, qkv_full, out_full, fc1_full, fc2_full = gather_parts(
        [packed, w_qkv.reshape(w_qkv.shape[0], -1), w_out, w_fc1, w_fc2],
        [True, True, False, True, False],
        line,
        1,
    )
    qkv_full = qkv_full.reshape((-1,) + w_qkv.shape[1:])
    fc1_full = fc1_full.reshape(-1, fc1_full.shape[-1])
    (
        gain_one,
        shift_one,
        bias_out,
        scale_one,
        gain_two,
        shift_two,
        bias_fc2,
        scale_two,
        bias_fc1,
    ) = [pack_full[:, i].reshape(-1) for i in range(9)]
    qv_width = qv_bias.shape[1]
    qv_full = pack_full[:, 9, : 2 * qv_width].reshape(owners, 2, qv_width)
    qv_full = qv_full.transpose(1, 0, 2).reshape(2, -1)
    mask_rows = mask_row.shape[0] // 128
    mask_part = lax.dynamic_slice_in_dim(pack_full, lax.axis_index("dp") * 2, 2, axis=0)
    full_mask = mask_part[:, 10 : 10 + mask_rows].reshape(-1)
    side = lax.axis_index("context")
    gain_one = gain_one.astype(jnp.float32)
    shift_one = shift_one.astype(jnp.float32)
    bias_out = bias_out.astype(jnp.float32)
    scale_one = scale_one.astype(jnp.float32)
    gain_two = gain_two.astype(jnp.float32)
    shift_two = shift_two.astype(jnp.float32)
    bias_fc1 = bias_fc1.astype(jnp.float32)
    bias_fc2 = bias_fc2.astype(jnp.float32)
    scale_two = scale_two.astype(jnp.float32)
    qv_float = qv_full.astype(jnp.float32)
    residual = tokens[0].astype(jnp.float32)
    row_count = residual.shape[0]
    model_width = residual.shape[1]
    local_width = qkv_full.shape[2]
    head_count = local_width // HEAD_DIM
    normed_one, inv_one = normalize(residual)
    hidden_one = (normed_one * gain_one + shift_one).astype(jnp.bfloat16)
    projected = jnp.dot(
        hidden_one,
        qkv_full.reshape(model_width, 3 * local_width),
        preferred_element_type=jnp.float32,
    ).reshape(row_count, 3, local_width)
    queries = (projected[:, 0] + qv_float[0]).astype(jnp.bfloat16)
    key_rows = projected[:, 1].astype(jnp.bfloat16)
    values = (projected[:, 2] + qv_float[1]).astype(jnp.bfloat16)
    query_heads = queries.reshape(row_count, head_count, HEAD_DIM)
    key_value = jnp.concatenate([key_rows, values], axis=1)
    other = swap(key_value, 2)
    pair = jnp.where(
        side == 0, jnp.concatenate([key_value, other]), jnp.concatenate([other, key_value])
    )
    back_keys, back_values = pair[:, :local_width], pair[:, local_width:]
    start_carry = (
        jnp.full((row_count, head_count, 1), NEGATIVE, jnp.float32),
        jnp.zeros((row_count, head_count, 1), jnp.float32),
        jnp.zeros((row_count, head_count, HEAD_DIM), jnp.float32),
    )
    running_max, running_total, running_sum = attend(
        start_carry,
        query_heads,
        back_keys,
        back_values,
        full_mask,
    )
    attn_heads = running_sum / running_total
    log_total = running_max + jnp.log(running_total)
    attended = attn_heads.reshape(row_count, local_width).astype(jnp.bfloat16)
    branch = (
        tensor_sum(
            [jnp.dot(attended, out_full, preferred_element_type=jnp.float32).astype(jnp.bfloat16)], 4
        )[0].astype(jnp.float32)
        + bias_out
    )
    residual_one = residual + scale_one * branch
    normed_two, inv_two = normalize(residual_one)
    hidden_two = (normed_two * gain_two + shift_two).astype(jnp.bfloat16)
    pre_act = jnp.dot(hidden_two, fc1_full, preferred_element_type=jnp.float32) + bias_fc1
    activated, gelu_pull = jax.vjp(lambda value: jax.nn.gelu(value, approximate=False), pre_act)
    hidden = activated.astype(jnp.bfloat16)
    mlp_part = jnp.dot(hidden, fc2_full, preferred_element_type=jnp.float32).astype(jnp.bfloat16)
    grad_out = cotangent[0].astype(jnp.float32)
    grad_mlp = (grad_out * scale_two).astype(jnp.bfloat16)
    grad_bias_fc2 = jnp.sum(grad_mlp.astype(jnp.float32), axis=0)
    grad_fc2 = contract_rows(hidden, grad_mlp)
    grad_act = contract_cols(grad_mlp, fc2_full)
    grad_pre = gelu_pull(grad_act)[0].astype(jnp.bfloat16)
    grad_bias_fc1 = jnp.sum(grad_pre.astype(jnp.float32), axis=0)
    grad_fc1 = contract_rows(hidden_two, grad_pre)
    grad_part = contract_cols(grad_pre, fc1_full).astype(jnp.bfloat16)
    grad_hidden_two, mlp_sum = tensor_sum([grad_part, mlp_part], 5)
    grad_hidden_two = grad_hidden_two.astype(jnp.float32)
    mlp_out = mlp_sum.astype(jnp.float32) + bias_fc2
    block_out = (residual_one + scale_two * mlp_out).astype(jnp.bfloat16)
    grad_scale_two = jnp.sum(grad_out * mlp_out, axis=0)
    grad_gain_two = jnp.sum(grad_hidden_two * normed_two, axis=0)
    grad_shift_two = jnp.sum(grad_hidden_two, axis=0)
    grad_residual_one = grad_out + norm_backward(grad_hidden_two, normed_two, inv_two, gain_two)
    grad_scale_one = jnp.sum(grad_residual_one * branch, axis=0)
    grad_branch = (grad_residual_one * scale_one).astype(jnp.bfloat16)
    grad_bias_out = jnp.sum(grad_branch.astype(jnp.float32), axis=0)
    grad_wout = contract_rows(attended, grad_branch)
    grad_attended = contract_cols(grad_branch, out_full).astype(jnp.bfloat16)
    grad_attn_heads = grad_attended.reshape(row_count, head_count, HEAD_DIM)
    row_delta = jnp.sum(grad_attn_heads.astype(jnp.float32) * attn_heads, axis=-1, keepdims=True)
    back_mask = full_mask
    key_count = back_keys.shape[0]
    grad_query = jnp.zeros((row_count, head_count, HEAD_DIM), jnp.float32)
    key_terms = []
    value_terms = []
    for offset in range(0, key_count, 512):
        finish = min(key_count, offset + 512)
        key_block = back_keys[offset:finish].reshape(finish - offset, head_count, HEAD_DIM)
        value_block = back_values[offset:finish].reshape(finish - offset, head_count, HEAD_DIM)
        mask_block = back_mask[offset:finish][None, None, :] > 0
        scores = jnp.einsum(
            "rhe,nhe->rhn", query_heads, key_block, preferred_element_type=jnp.float32
        ) * HEAD_DIM ** (-0.5)
        attn_prob = jnp.where(mask_block, jnp.exp(scores - log_total), 0.0)
        value_terms.append(
            jnp.einsum(
                "rhn,rhe->nhe",
                attn_prob.astype(jnp.bfloat16),
                grad_attn_heads,
                preferred_element_type=jnp.float32,
            )
        )
        grad_prob = jnp.einsum(
            "rhe,nhe->rhn", grad_attn_heads, value_block, preferred_element_type=jnp.float32
        )
        grad_scores = (attn_prob * (grad_prob - row_delta)).astype(jnp.bfloat16)
        grad_query = grad_query + jnp.einsum(
            "rhn,nhe->rhe", grad_scores, key_block, preferred_element_type=jnp.float32
        ) * HEAD_DIM ** (-0.5)
        key_terms.append(
            jnp.einsum("rhn,rhe->nhe", grad_scores, query_heads, preferred_element_type=jnp.float32)
            * HEAD_DIM ** (-0.5)
        )
    key_sums = jnp.concatenate(key_terms, axis=0).reshape(key_count, local_width)
    value_sums = jnp.concatenate(value_terms, axis=0).reshape(key_count, local_width)
    sums = jnp.concatenate([key_sums, value_sums], axis=1)
    away = lax.dynamic_slice_in_dim(sums, (1 - side) * row_count, row_count, axis=0)
    home = lax.dynamic_slice_in_dim(sums, side * row_count, row_count, axis=0)
    home = home + swap(away.astype(jnp.bfloat16), 3).astype(jnp.float32)
    grad_keys, grad_values = home[:, :local_width], home[:, local_width:]
    grad_projected = jnp.stack(
        [grad_query.reshape(row_count, local_width), grad_keys, grad_values], axis=1
    ).astype(jnp.bfloat16)
    grad_float = grad_projected.astype(jnp.float32)
    grad_qv = jnp.stack(
        [jnp.sum(grad_float[:, 0], axis=0), jnp.sum(grad_float[:, 2], axis=0)], axis=0
    )
    grad_flat = grad_projected.reshape(row_count, 3 * local_width)
    grad_qkv = contract_rows(hidden_one, grad_flat)
    grad_hidden_one = tensor_sum(
        [
            contract_cols(grad_flat, qkv_full.reshape(model_width, 3 * local_width)).astype(
                jnp.bfloat16
            )
        ],
        6,
    )[0].astype(jnp.float32)
    grad_gain_one = jnp.sum(grad_hidden_one * normed_one, axis=0)
    grad_shift_one = jnp.sum(grad_hidden_one, axis=0)
    token_grad = grad_residual_one + norm_backward(grad_hidden_one, normed_one, inv_one, gain_one)
    qv_rows = grad_qv.reshape(2, owners, qv_width).transpose(1, 0, 2)
    grad_pack = pack_rows(
        [
            grad_gain_one,
            grad_shift_one,
            grad_bias_out,
            grad_scale_one,
            grad_gain_two,
            grad_shift_two,
            grad_bias_fc2,
            grad_scale_two,
            grad_bias_fc1,
            qv_rows,
        ],
        owners,
        jnp.float32,
    )
    pack_sum, qkv_sum, out_sum, fc1_sum, fc2_sum = scatter_parts(
        [
            grad_pack,
            grad_qkv.astype(jnp.bfloat16).reshape(owners, -1, 3 * local_width),
            grad_wout.astype(jnp.bfloat16),
            grad_fc1.astype(jnp.bfloat16).reshape(owners, -1, grad_fc1.shape[1]),
            grad_fc2.astype(jnp.bfloat16),
        ],
        line,
        7,
    )
    return (
        block_out[None],
        token_grad[None],
        pack_sum[0],
        pack_sum[1],
        qkv_sum.reshape(w_qkv.shape),
        pack_sum[9, : 2 * qv_width].reshape(2, qv_width),
        out_sum,
        pack_sum[2],
        pack_sum[3],
        pack_sum[4],
        pack_sum[5],
        fc1_sum,
        pack_sum[8],
        fc2_sum,
        pack_sum[6],
        pack_sum[7],
    )


def solution(mesh):
    line = mesh.shape["dp"]
    own_kernels = mesh.shape["context"] == 2 and mesh.shape["tensor"] == 4 and line == 4
    return jax.shard_map(
        functools.partial(on_device_line, line) if own_kernels else on_device,
        mesh=mesh,
        in_specs=(
            P("dp", "context", None),
            P("dp", "context"),
            P(("dp", "context")),
            P(("dp", "context")),
            P(("dp", "context"), None, "tensor"),
            P(None, ("tensor", "dp", "context")),
            P("tensor", ("dp", "context")),
            P(("dp", "context")),
            P(("dp", "context")),
            P(("dp", "context")),
            P(("dp", "context")),
            P(("dp", "context"), "tensor"),
            P(("tensor", "dp", "context")),
            P("tensor", ("dp", "context")),
            P(("dp", "context")),
            P(("dp", "context")),
            P("dp", "context", None),
        ),
        out_specs=(
            P("dp", "context", None),
            P("dp", "context", None),
            P(("dp", "context")),
            P(("dp", "context")),
            P(("dp", "context"), None, "tensor"),
            P(None, ("tensor", "dp", "context")),
            P("tensor", ("dp", "context")),
            P(("dp", "context")),
            P(("dp", "context")),
            P(("dp", "context")),
            P(("dp", "context")),
            P(("dp", "context"), "tensor"),
            P(("tensor", "dp", "context")),
            P("tensor", ("dp", "context")),
            P(("dp", "context")),
            P(("dp", "context")),
        ),
        check_vma=False,
    )
```

```python
import functools
import math

import jax
import jax.numpy as jnp
from jax import lax
from jax.experimental import pallas as pl
from jax.experimental.pallas import tpu as pltpu
from jax.sharding import PartitionSpec as P

HEAD_DIM = 64
MESH = pl.DeviceIdType.MESH
VMEM_LIMIT = 56 * 1024 * 1024

EPSILON = 1e-06
NEGATIVE = -1e30


def normalize(value):
    average = jnp.mean(value, axis=-1, keepdims=True)
    centred = value - average
    inv_std = lax.rsqrt(jnp.mean(centred * centred, axis=-1, keepdims=True) + EPSILON)
    return (centred * inv_std, inv_std)


def norm_backward(grad_norm, normed, inv_std, gain):
    scaled = grad_norm * gain
    return (
        scaled
        - jnp.mean(scaled, axis=-1, keepdims=True)
        - normed * jnp.mean(scaled * normed, axis=-1, keepdims=True)
    ) * inv_std


def contract_rows(first_matrix, second_matrix):
    return lax.dot_general(
        first_matrix, second_matrix, (((0,), (0,)), ((), ())), preferred_element_type=jnp.float32
    )


def contract_cols(first_matrix, second_matrix):
    return lax.dot_general(
        first_matrix, second_matrix, (((1,), (1,)), ((), ())), preferred_element_type=jnp.float32
    )


def attend(carry, query_heads, key_rows, value_rows, key_mask):
    running_max, running_total, running_sum = carry
    key_count = key_rows.shape[0]
    head_count = query_heads.shape[1]
    for offset in range(0, key_count, 512):
        finish = min(key_count, offset + 512)
        key_block = key_rows[offset:finish].reshape(finish - offset, head_count, HEAD_DIM)
        value_block = value_rows[offset:finish].reshape(finish - offset, head_count, HEAD_DIM)
        mask_block = key_mask[offset:finish][None, None, :] > 0
        scores = jnp.einsum(
            "rhe,nhe->rhn", query_heads, key_block, preferred_element_type=jnp.float32
        ) * HEAD_DIM ** (-0.5)
        scores = jnp.where(mask_block, scores, NEGATIVE)
        new_max = jnp.maximum(running_max, jnp.max(scores, axis=-1, keepdims=True))
        weights = jnp.where(mask_block, jnp.exp(scores - new_max), 0.0)
        factor = jnp.exp(running_max - new_max)
        running_total = running_total * factor + jnp.sum(weights, axis=-1, keepdims=True)
        running_sum = running_sum * factor + jnp.einsum(
            "rhn,nhe->rhe",
            weights.astype(jnp.bfloat16),
            value_block,
            preferred_element_type=jnp.float32,
        )
        running_max = new_max
    return (running_max, running_total, running_sum)


def params(ident):
    return pltpu.CompilerParams(
        collective_id=ident, has_side_effects=True, vmem_limit_bytes=VMEM_LIMIT
    )


def greet(count, device_id):
    pl.semaphore_signal(
        pltpu.get_barrier_semaphore(), inc=count, device_id=device_id, device_id_type=MESH
    )


def remote(src, dst, send_sem, recv_sem, device_id):
    return pltpu.make_async_remote_copy(
        src_ref=src,
        dst_ref=dst,
        send_sem=send_sem,
        recv_sem=recv_sem,
        device_id=device_id,
        device_id_type=MESH,
    )


def greet_line(line):
    here = lax.axis_index("dp")
    side = lax.axis_index("context")
    greet(1, {"context": 1 - side})

    @pl.when(here < line - 1)
    def _():
        greet(1, {"dp": here + 1})

    @pl.when(here > 0)
    def _():
        greet(1, {"dp": here - 1})

    above = jnp.where(here < line - 1, 1, 0)
    below = jnp.where(here > 0, 1, 0)
    pl.semaphore_wait(pltpu.get_barrier_semaphore(), 1 + above + below)


def owner_view(ref, owner, width):
    if len(ref.shape) == 3:
        return ref.at[owner]
    return ref.at[:, pl.ds(pl.multiple_of(owner * width, width), width)]


def attend_head(head, query_ref, near_ref, far_ref, near_mask, far_mask, attn_ref, log_ref):
    rows, width = query_ref.shape
    block = math.gcd(rows, 256)
    at = slice(head * HEAD_DIM, (head + 1) * HEAD_DIM)
    value_at = slice(width + head * HEAD_DIM, width + (head + 1) * HEAD_DIM)

    def body(i, carry):
        rows_at = pl.ds(pl.multiple_of(i * block, block), block)
        query = query_ref[rows_at, at]
        near = contract_cols(query, near_ref[:, at]) * HEAD_DIM ** (-0.5)
        far = contract_cols(query, far_ref[:, at]) * HEAD_DIM ** (-0.5)
        near = jnp.where(near_mask[...] > 0, near, NEGATIVE)
        far = jnp.where(far_mask[...] > 0, far, NEGATIVE)
        highest = jnp.maximum(
            jnp.max(near, axis=-1, keepdims=True), jnp.max(far, axis=-1, keepdims=True)
        )
        near = jnp.exp(near - highest)
        far = jnp.exp(far - highest)
        total = jnp.sum(near, axis=-1, keepdims=True) + jnp.sum(far, axis=-1, keepdims=True)
        out = jnp.dot(
            near.astype(jnp.bfloat16), near_ref[:, value_at], preferred_element_type=jnp.float32
        ) + jnp.dot(
            far.astype(jnp.bfloat16), far_ref[:, value_at], preferred_element_type=jnp.float32
        )
        attn_ref[rows_at, at] = out / total
        log_ref[rows_at, head : head + 1] = highest + jnp.log(total)
        return carry

    lax.fori_loop(0, rows // block, body, 0)


def gather_kernel(line, count, attend_too, *refs):
    extra_in = 4 if attend_too else 0
    extra_out = 3 if attend_too else 0
    ins, rest = refs[:count], refs[count:]
    given, rest = rest[:extra_in], rest[extra_in:]
    outs, rest = rest[:count], rest[count:]
    made, rest = rest[:extra_out], rest[extra_out:]
    send, recv, local = rest[:3]
    here = lax.axis_index("dp")
    side = lax.axis_index("context")
    cross = 2 * (line - 1)

    def part(a, row, column):
        return owner_view(outs[a], row * 2 + column, ins[a].shape[-1])

    def up(a, s, row):
        src = ins[a] if s == 0 else part(a, row, side)
        return remote(
            src, part(a, row, side), send.at[a, s], recv.at[a, s], {"dp": here + 1}
        )

    def down(a, s, row):
        src = ins[a] if s == 0 else part(a, row, side)
        slot = line - 1 + s
        return remote(
            src, part(a, row, side), send.at[a, slot], recv.at[a, slot], {"dp": here - 1}
        )

    def over(a, row, own):
        src = ins[a] if own else part(a, row, side)
        return remote(
            src,
            part(a, row, side),
            send.at[a, cross + row],
            recv.at[a, cross + row],
            {"context": 1 - side},
        )

    greet_line(line)
    heads = []
    if attend_too:
        query_ref, near_ref, near_mask, far_mask = given
        far_ref, attn_ref, log_ref = made
        swap_copy = remote(near_ref, far_ref, rest[3], rest[4], {"context": 1 - side})
        swap_copy.start()
        heads = list(range(query_ref.shape[1] // HEAD_DIM))
    for a in range(count):

        @pl.when(here < line - 1)
        def _():
            up(a, 0, here).start()

        @pl.when(here > 0)
        def _():
            down(a, 0, here).start()

        over(a, here, True).start()
        pltpu.make_async_copy(ins[a], part(a, here, side), local.at[a]).start()
    for s in range(1, line):
        for a in range(count):

            @pl.when(here - s >= 0)
            def _():
                up(a, s - 1, here - s).wait_recv()

                @pl.when(here < line - 1)
                def _():
                    up(a, s, here - s).start()

                over(a, here - s, False).start()

            @pl.when(here + s <= line - 1)
            def _():
                down(a, s - 1, here + s).wait_recv()

                @pl.when(here > 0)
                def _():
                    down(a, s, here + s).start()

                over(a, here + s, False).start()

        if attend_too and s == 1:
            swap_copy.wait()
        now = heads[:2] if s < line - 1 else heads
        heads = heads[len(now) :]
        for head in now:
            attend_head(
                head, query_ref, near_ref, far_ref, near_mask, far_mask, attn_ref, log_ref
            )

    for a in range(count):
        pltpu.make_async_copy(ins[a], part(a, here, side), local.at[a]).wait()
        for row in range(line):
            remote(
                part(a, row, 1 - side),
                part(a, row, 1 - side),
                send.at[a, cross + row],
                recv.at[a, cross + row],
                {"context": 1 - side},
            ).wait_recv()
            over(a, row, False).wait_send()
        for s in range(line - 1):

            @pl.when((here < line - 1) & (here - s >= 0))
            def _():
                up(a, s, here - s).wait_send()

            @pl.when((here > 0) & (here + s <= line - 1))
            def _():
                down(a, s, here + s).wait_send()


def gather_parts(arrays, stacked, line, ident, attend_args=()):
    owners = line * 2
    shapes = []
    for array, stack in zip(arrays, stacked):
        if stack:
            shape = (owners,) + array.shape
        else:
            shape = (array.shape[0], owners * array.shape[1])
        shapes.append(jax.ShapeDtypeStruct(shape, array.dtype))
    count = len(arrays)
    slots = 2 * (line - 1) + line
    anywhere = pl.BlockSpec(memory_space=pl.ANY)
    in_vmem = pl.BlockSpec(memory_space=pltpu.VMEM)
    extra_shapes = []
    extra_sems = []
    if attend_args:
        query, key_value = attend_args[:2]
        extra_shapes = [
            jax.ShapeDtypeStruct(key_value.shape, key_value.dtype),
            jax.ShapeDtypeStruct(query.shape, jnp.float32),
            jax.ShapeDtypeStruct((query.shape[0], 128), jnp.float32),
        ]
        extra_sems = [pltpu.SemaphoreType.DMA, pltpu.SemaphoreType.DMA]
    return pl.pallas_call(
        functools.partial(gather_kernel, line, count, bool(attend_args)),
        out_shape=tuple(shapes + extra_shapes),
        in_specs=[anywhere] * count + [in_vmem] * len(attend_args),
        out_specs=tuple([anywhere] * count + [in_vmem] * len(extra_shapes)),
        scratch_shapes=[
            pltpu.SemaphoreType.DMA((count, slots)),
            pltpu.SemaphoreType.DMA((count, slots)),
            pltpu.SemaphoreType.DMA((count,)),
        ]
        + extra_sems,
        compiler_params=params(ident),
    )(*arrays, *attend_args)


def swap_kernel(in_ref, out_ref, send, recv):
    side = lax.axis_index("context")
    greet(1, {"context": 1 - side})
    pl.semaphore_wait(pltpu.get_barrier_semaphore(), 1)
    copy = remote(in_ref, out_ref, send, recv, {"context": 1 - side})
    copy.start()
    copy.wait()


def swap(array, ident):
    return pl.pallas_call(
        swap_kernel,
        out_shape=jax.ShapeDtypeStruct(array.shape, array.dtype),
        in_specs=[pl.BlockSpec(memory_space=pl.ANY)],
        out_specs=pl.BlockSpec(memory_space=pl.ANY),
        scratch_shapes=[pltpu.SemaphoreType.DMA, pltpu.SemaphoreType.DMA],
        compiler_params=params(ident),
    )(array)


PIECES = 4


def tensor_sum_kernel(count, *refs):
    ins, outs = refs[:count], refs[count : 2 * count]
    pair_buf, sum_buf, far_buf, send, recv = refs[2 * count :]
    place = lax.axis_index("tensor")
    core = lax.rem(place, 2)
    pair = {"tensor": place + 1 - 2 * core}
    far = {"tensor": lax.rem(place + 2, 4)}
    greet(1, pair)
    greet(1, far)
    pl.semaphore_wait(pltpu.get_barrier_semaphore(), 2)
    half = ins[0].shape[0] // 2
    step = half // PIECES

    def rows(which, p):
        return pl.ds(pl.multiple_of(which * half + p * step, step), step)

    def first(a, p):
        return remote(
            ins[a].at[rows(1 - core, p)],
            pair_buf.at[a, p],
            send.at[0, a, p],
            recv.at[0, a, p],
            pair,
        )

    def second(a, p):
        return remote(
            sum_buf.at[a, p], far_buf.at[a, p], send.at[1, a, p], recv.at[1, a, p], far
        )

    def third(a, p):
        return remote(
            outs[a].at[rows(core, p)],
            outs[a].at[rows(core, p)],
            send.at[2, a, p],
            recv.at[2, a, p],
            pair,
        )

    todo = [(a, p) for a in range(count) for p in range(PIECES)]
    for a, p in todo:
        first(a, p).start()
    for a, p in todo:
        first(a, p).wait_recv()
        total = ins[a][rows(core, p), :].astype(jnp.float32) + pair_buf[a, p].astype(jnp.float32)
        sum_buf[a, p] = total.astype(jnp.bfloat16)
        second(a, p).start()
    for a, p in todo:
        second(a, p).wait_recv()
        total = sum_buf[a, p].astype(jnp.float32) + far_buf[a, p].astype(jnp.float32)
        outs[a][rows(core, p), :] = total.astype(jnp.bfloat16)
        third(a, p).start()
    for a, p in todo:
        remote(
            outs[a].at[rows(1 - core, p)],
            outs[a].at[rows(1 - core, p)],
            send.at[2, a, p],
            recv.at[2, a, p],
            pair,
        ).wait_recv()
        first(a, p).wait_send()
        second(a, p).wait_send()
        third(a, p).wait_send()


def tensor_sum(arrays, ident):
    count = len(arrays)
    rows, width = arrays[0].shape
    buf = pltpu.VMEM((count, PIECES, rows // 2 // PIECES, width), jnp.bfloat16)
    return pl.pallas_call(
        functools.partial(tensor_sum_kernel, count),
        out_shape=tuple(jax.ShapeDtypeStruct(a.shape, a.dtype) for a in arrays),
        in_specs=[pl.BlockSpec(memory_space=pltpu.VMEM)] * count,
        out_specs=tuple([pl.BlockSpec(memory_space=pltpu.VMEM)] * count),
        scratch_shapes=[
            buf,
            buf,
            buf,
            pltpu.SemaphoreType.DMA((3, count, PIECES)),
            pltpu.SemaphoreType.DMA((3, count, PIECES)),
        ],
        compiler_params=params(ident),
    )(*arrays)


def add_rows(dst, terms):
    count, width = dst.shape
    block = math.gcd(count, 64 if width > 512 else 256)

    def body(i, carry):
        at = pl.ds(pl.multiple_of(i * block, block), block)
        total = terms[0][at, :].astype(jnp.float32)
        for term in terms[1:]:
            total = total + term[at, :].astype(jnp.float32)
        dst[at, :] = total.astype(dst.dtype)
        return carry

    lax.fori_loop(0, count // block, body, 0)


def scatter_kernel(line, count, *refs):
    ins, outs = refs[:count], refs[count : 2 * count]
    cross = refs[2 * count : 3 * count]
    climb = refs[3 * count : 4 * count]
    fall = refs[4 * count : 5 * count]
    send, recv = refs[5 * count :]
    here = lax.axis_index("dp")
    side = lax.axis_index("context")

    def mine(a, row, column):
        return owner_view(ins[a], row * 2 + column, outs[a].shape[-1])

    def over(a, row):
        return remote(
            mine(a, row, 1 - side),
            cross[a].at[row],
            send.at[0, a, row],
            recv.at[0, a, row],
            {"context": 1 - side},
        )

    def up(a, row):
        return remote(
            cross[a].at[row],
            climb[a].at[row],
            send.at[1, a, row],
            recv.at[1, a, row],
            {"dp": here + 1},
        )

    def down(a, row):
        return remote(
            cross[a].at[row],
            fall[a].at[row],
            send.at[2, a, row],
            recv.at[2, a, row],
            {"dp": here - 1},
        )

    greet_line(line)
    order = [
        jnp.where(here < 2, 3, 0),
        jnp.where(here == 0, 2, jnp.where(here == 1, 0, jnp.where(here == 2, 3, 1))),
        jnp.where(here == 0, 1, jnp.where(here == 1, 2, jnp.where(here == 2, 1, 2))),
        here,
    ]
    for row in order:
        for a in range(count):
            over(a, row).start()
    for k in range(line - 1):
        for a in range(count):
            high, low = line - 1 - k, k

            @pl.when(here < high)
            def _():
                over(a, high).wait_recv()

                @pl.when(here == 0)
                def _():
                    add_rows(cross[a].at[high], [mine(a, high, side), cross[a].at[high]])

                @pl.when(here > 0)
                def _():
                    up(a, high).wait_recv()
                    add_rows(
                        cross[a].at[high],
                        [mine(a, high, side), cross[a].at[high], climb[a].at[high]],
                    )

                up(a, high).start()

            @pl.when(here > low)
            def _():
                over(a, low).wait_recv()

                @pl.when(here == line - 1)
                def _():
                    add_rows(cross[a].at[low], [mine(a, low, side), cross[a].at[low]])

                @pl.when(here < line - 1)
                def _():
                    down(a, low).wait_recv()
                    add_rows(
                        cross[a].at[low],
                        [mine(a, low, side), cross[a].at[low], fall[a].at[low]],
                    )

                down(a, low).start()

    for a in range(count):
        over(a, here).wait_recv()
        own = [mine(a, here, side), cross[a].at[here]]

        @pl.when(here == 0)
        def _():
            down(a, here).wait_recv()
            add_rows(outs[a], own + [fall[a].at[here]])

        @pl.when(here == line - 1)
        def _():
            up(a, here).wait_recv()
            add_rows(outs[a], own + [climb[a].at[here]])

        @pl.when((here > 0) & (here < line - 1))
        def _():
            down(a, here).wait_recv()
            up(a, here).wait_recv()
            add_rows(outs[a], own + [climb[a].at[here], fall[a].at[here]])

    for a in range(count):
        for row in range(line):
            over(a, row).wait_send()

            @pl.when(here < row)
            def _():
                up(a, row).wait_send()

            @pl.when(here > row)
            def _():
                down(a, row).wait_send()


def scatter_parts(arrays, line, ident):
    owners = 2 * line
    count = len(arrays)
    outs = []
    for array in arrays:
        if array.ndim == 3:
            outs.append(array.shape[1:])
        else:
            outs.append((array.shape[0], array.shape[1] // owners))
    bufs = [pltpu.VMEM((line,) + o, a.dtype) for o, a in zip(outs, arrays)]
    return pl.pallas_call(
        functools.partial(scatter_kernel, line, count),
        out_shape=tuple(jax.ShapeDtypeStruct(o, jnp.float32) for o in outs),
        in_specs=[pl.BlockSpec(memory_space=pltpu.VMEM)] * count,
        out_specs=tuple([pl.BlockSpec(memory_space=pltpu.VMEM)] * count),
        scratch_shapes=bufs * 3
        + [pltpu.SemaphoreType.DMA((3, count, line)), pltpu.SemaphoreType.DMA((3, count, line))],
        compiler_params=params(ident),
    )(*arrays)


def pack_rows(vectors, owners, dtype):
    rows = [v.reshape(owners, -1).astype(dtype) for v in vectors]
    rows = [jnp.pad(r, ((0, 0), (0, -r.shape[1] % 128))).reshape(owners, -1, 128) for r in rows]
    packed = jnp.concatenate(rows, axis=1)
    return jnp.pad(packed, ((0, 0), (0, 16 - packed.shape[1]), (0, 0)))

def on_device(
    tokens,
    key_valid,
    norm1_gain,
    norm1_shift,
    w_qkv,
    qv_bias,
    w_out,
    out_bias,
    scale1,
    norm2_gain,
    norm2_shift,
    w_fc1,
    fc1_bias,
    w_fc2,
    fc2_bias,
    scale2,
    cotangent,
):
    gathered = (
        lax.all_gather(norm1_gain, ("dp", "context"), axis=0, tiled=True),
        lax.all_gather(norm1_shift, ("dp", "context"), axis=0, tiled=True),
        lax.all_gather(w_qkv, ("dp", "context"), axis=0, tiled=True),
        lax.all_gather(qv_bias, ("dp", "context"), axis=1, tiled=True),
        lax.all_gather(w_out, ("dp", "context"), axis=1, tiled=True),
        lax.all_gather(out_bias, ("dp", "context"), axis=0, tiled=True),
        lax.all_gather(scale1, ("dp", "context"), axis=0, tiled=True),
        lax.all_gather(norm2_gain, ("dp", "context"), axis=0, tiled=True),
        lax.all_gather(norm2_shift, ("dp", "context"), axis=0, tiled=True),
        lax.all_gather(w_fc1, ("dp", "context"), axis=0, tiled=True),
        lax.all_gather(fc1_bias, ("dp", "context"), axis=0, tiled=True),
        lax.all_gather(w_fc2, ("dp", "context"), axis=1, tiled=True),
        lax.all_gather(fc2_bias, ("dp", "context"), axis=0, tiled=True),
        lax.all_gather(scale2, ("dp", "context"), axis=0, tiled=True),
    )
    (
        gain_one,
        shift_one,
        qkv_full,
        qv_full,
        out_full,
        bias_out,
        scale_one,
        gain_two,
        shift_two,
        fc1_full,
        bias_fc1,
        fc2_full,
        bias_fc2,
        scale_two,
    ) = gathered
    gain_one = gain_one.astype(jnp.float32)
    shift_one = shift_one.astype(jnp.float32)
    bias_out = bias_out.astype(jnp.float32)
    scale_one = scale_one.astype(jnp.float32)
    gain_two = gain_two.astype(jnp.float32)
    shift_two = shift_two.astype(jnp.float32)
    bias_fc1 = bias_fc1.astype(jnp.float32)
    bias_fc2 = bias_fc2.astype(jnp.float32)
    scale_two = scale_two.astype(jnp.float32)
    qv_float = qv_full.astype(jnp.float32)
    residual = tokens[0].astype(jnp.float32)
    row_count = residual.shape[0]
    model_width = residual.shape[1]
    local_width = qkv_full.shape[2]
    head_count = local_width // HEAD_DIM
    normed_one, inv_one = normalize(residual)
    hidden_one = (normed_one * gain_one + shift_one).astype(jnp.bfloat16)
    projected = jnp.dot(
        hidden_one,
        qkv_full.reshape(model_width, 3 * local_width),
        preferred_element_type=jnp.float32,
    ).reshape(row_count, 3, local_width)
    queries = (projected[:, 0] + qv_float[0]).astype(jnp.bfloat16)
    key_rows = projected[:, 1].astype(jnp.bfloat16)
    values = (projected[:, 2] + qv_float[1]).astype(jnp.bfloat16)
    query_heads = queries.reshape(row_count, head_count, HEAD_DIM)
    key_mask = key_valid[0].astype(jnp.bfloat16)
    start_carry = (
        jnp.full((row_count, head_count, 1), NEGATIVE, jnp.float32),
        jnp.zeros((row_count, head_count, 1), jnp.float32),
        jnp.zeros((row_count, head_count, HEAD_DIM), jnp.float32),
    )
    running_max, running_total, running_sum = attend(
        start_carry,
        query_heads,
        lax.all_gather(key_rows, "context", axis=0, tiled=True),
        lax.all_gather(values, "context", axis=0, tiled=True),
        lax.all_gather(key_mask, "context", axis=0, tiled=True),
    )
    attn_heads = running_sum / running_total
    log_total = running_max + jnp.log(running_total)
    attended = attn_heads.reshape(row_count, local_width).astype(jnp.bfloat16)
    branch = (
        lax.psum(
            jnp.dot(attended, out_full, preferred_element_type=jnp.float32).astype(jnp.bfloat16),
            "tensor",
        ).astype(jnp.float32)
        + bias_out
    )
    residual_one = residual + scale_one * branch
    normed_two, inv_two = normalize(residual_one)
    hidden_two = (normed_two * gain_two + shift_two).astype(jnp.bfloat16)
    pre_act = jnp.dot(hidden_two, fc1_full, preferred_element_type=jnp.float32) + bias_fc1
    activated, gelu_pull = jax.vjp(lambda value: jax.nn.gelu(value, approximate=False), pre_act)
    hidden = activated.astype(jnp.bfloat16)
    mlp_out = (
        lax.psum(
            jnp.dot(hidden, fc2_full, preferred_element_type=jnp.float32).astype(jnp.bfloat16),
            "tensor",
        ).astype(jnp.float32)
        + bias_fc2
    )
    block_out = (residual_one + scale_two * mlp_out).astype(jnp.bfloat16)
    back_weights = (
        lax.all_gather(w_qkv, ("dp", "context"), axis=0, tiled=True),
        lax.all_gather(w_out, ("dp", "context"), axis=1, tiled=True),
        lax.all_gather(w_fc1, ("dp", "context"), axis=0, tiled=True),
        lax.all_gather(w_fc2, ("dp", "context"), axis=1, tiled=True),
    )
    qkv_back, out_back, fc1_back, fc2_back = back_weights
    grad_out = cotangent[0].astype(jnp.float32)
    grad_scale_two = jnp.sum(grad_out * mlp_out, axis=0)
    grad_mlp = (grad_out * scale_two).astype(jnp.bfloat16)
    grad_bias_fc2 = jnp.sum(grad_mlp.astype(jnp.float32), axis=0)
    grad_fc2 = contract_rows(hidden, grad_mlp)
    grad_act = contract_cols(grad_mlp, fc2_back)
    grad_pre = gelu_pull(grad_act)[0].astype(jnp.bfloat16)
    grad_bias_fc1 = jnp.sum(grad_pre.astype(jnp.float32), axis=0)
    grad_fc1 = contract_rows(hidden_two, grad_pre)
    grad_hidden_two = lax.psum(
        contract_cols(grad_pre, fc1_back).astype(jnp.bfloat16), "tensor"
    ).astype(jnp.float32)
    grad_gain_two = jnp.sum(grad_hidden_two * normed_two, axis=0)
    grad_shift_two = jnp.sum(grad_hidden_two, axis=0)
    grad_residual_one = grad_out + norm_backward(grad_hidden_two, normed_two, inv_two, gain_two)
    grad_scale_one = jnp.sum(grad_residual_one * branch, axis=0)
    grad_branch = (grad_residual_one * scale_one).astype(jnp.bfloat16)
    grad_bias_out = jnp.sum(grad_branch.astype(jnp.float32), axis=0)
    grad_wout = contract_rows(attended, grad_branch)
    grad_attended = contract_cols(grad_branch, out_back).astype(jnp.bfloat16)
    grad_attn_heads = grad_attended.reshape(row_count, head_count, HEAD_DIM)
    row_delta = jnp.sum(grad_attn_heads.astype(jnp.float32) * attn_heads, axis=-1, keepdims=True)
    back_keys, back_values, back_mask = (
        lax.all_gather(key_rows, "context", axis=0, tiled=True),
        lax.all_gather(values, "context", axis=0, tiled=True),
        lax.all_gather(key_mask, "context", axis=0, tiled=True),
    )
    key_count = back_keys.shape[0]
    grad_query = jnp.zeros((row_count, head_count, HEAD_DIM), jnp.float32)
    key_terms = []
    value_terms = []
    for offset in range(0, key_count, 512):
        finish = min(key_count, offset + 512)
        key_block = back_keys[offset:finish].reshape(finish - offset, head_count, HEAD_DIM)
        value_block = back_values[offset:finish].reshape(finish - offset, head_count, HEAD_DIM)
        mask_block = back_mask[offset:finish][None, None, :] > 0
        scores = jnp.einsum(
            "rhe,nhe->rhn", query_heads, key_block, preferred_element_type=jnp.float32
        ) * HEAD_DIM ** (-0.5)
        attn_prob = jnp.where(mask_block, jnp.exp(scores - log_total), 0.0)
        value_terms.append(
            jnp.einsum(
                "rhn,rhe->nhe",
                attn_prob.astype(jnp.bfloat16),
                grad_attn_heads,
                preferred_element_type=jnp.float32,
            )
        )
        grad_prob = jnp.einsum(
            "rhe,nhe->rhn", grad_attn_heads, value_block, preferred_element_type=jnp.float32
        )
        grad_scores = (attn_prob * (grad_prob - row_delta)).astype(jnp.bfloat16)
        grad_query = grad_query + jnp.einsum(
            "rhn,nhe->rhe", grad_scores, key_block, preferred_element_type=jnp.float32
        ) * HEAD_DIM ** (-0.5)
        key_terms.append(
            jnp.einsum("rhn,rhe->nhe", grad_scores, query_heads, preferred_element_type=jnp.float32)
            * HEAD_DIM ** (-0.5)
        )
    key_sums = jnp.concatenate(key_terms, axis=0).reshape(key_count, local_width)
    value_sums = jnp.concatenate(value_terms, axis=0).reshape(key_count, local_width)
    grad_keys, grad_values = (
        lax.psum_scatter(
            key_sums.astype(jnp.bfloat16), "context", scatter_dimension=0, tiled=True
        ).astype(jnp.float32),
        lax.psum_scatter(
            value_sums.astype(jnp.bfloat16), "context", scatter_dimension=0, tiled=True
        ).astype(jnp.float32),
    )
    grad_projected = jnp.stack(
        [grad_query.reshape(row_count, local_width), grad_keys, grad_values], axis=1
    ).astype(jnp.bfloat16)
    grad_float = grad_projected.astype(jnp.float32)
    grad_qv = jnp.stack(
        [jnp.sum(grad_float[:, 0], axis=0), jnp.sum(grad_float[:, 2], axis=0)], axis=0
    )
    grad_flat = grad_projected.reshape(row_count, 3 * local_width)
    grad_qkv = contract_rows(hidden_one, grad_flat).reshape(model_width, 3, local_width)
    grad_hidden_one = lax.psum(
        contract_cols(grad_flat, qkv_back.reshape(model_width, 3 * local_width)).astype(
            jnp.bfloat16
        ),
        "tensor",
    ).astype(jnp.float32)
    grad_gain_one = jnp.sum(grad_hidden_one * normed_one, axis=0)
    grad_shift_one = jnp.sum(grad_hidden_one, axis=0)
    token_grad = grad_residual_one + norm_backward(grad_hidden_one, normed_one, inv_one, gain_one)
    shards = (
        lax.psum_scatter(grad_gain_one, ("dp", "context"), scatter_dimension=0, tiled=True),
        lax.psum_scatter(grad_shift_one, ("dp", "context"), scatter_dimension=0, tiled=True),
        lax.psum_scatter(grad_qkv, ("dp", "context"), scatter_dimension=0, tiled=True),
        lax.psum_scatter(grad_qv, ("dp", "context"), scatter_dimension=1, tiled=True),
        lax.psum_scatter(grad_wout, ("dp", "context"), scatter_dimension=1, tiled=True),
        lax.psum_scatter(grad_bias_out, ("dp", "context"), scatter_dimension=0, tiled=True),
        lax.psum_scatter(grad_scale_one, ("dp", "context"), scatter_dimension=0, tiled=True),
        lax.psum_scatter(grad_gain_two, ("dp", "context"), scatter_dimension=0, tiled=True),
        lax.psum_scatter(grad_shift_two, ("dp", "context"), scatter_dimension=0, tiled=True),
        lax.psum_scatter(grad_fc1, ("dp", "context"), scatter_dimension=0, tiled=True),
        lax.psum_scatter(grad_bias_fc1, ("dp", "context"), scatter_dimension=0, tiled=True),
        lax.psum_scatter(grad_fc2, ("dp", "context"), scatter_dimension=1, tiled=True),
        lax.psum_scatter(grad_bias_fc2, ("dp", "context"), scatter_dimension=0, tiled=True),
        lax.psum_scatter(grad_scale_two, ("dp", "context"), scatter_dimension=0, tiled=True),
    )
    return (block_out[None], token_grad[None]) + tuple(shards)


def on_device_line(
    line,
    tokens,
    key_valid,
    norm1_gain,
    norm1_shift,
    w_qkv,
    qv_bias,
    w_out,
    out_bias,
    scale1,
    norm2_gain,
    norm2_shift,
    w_fc1,
    fc1_bias,
    w_fc2,
    fc2_bias,
    scale2,
    cotangent,
):
    owners = 2 * line
    mask_row = key_valid[0].astype(jnp.bfloat16)
    packed = pack_rows(
        [
            norm1_gain,
            norm1_shift,
            out_bias,
            scale1,
            norm2_gain,
            norm2_shift,
            fc2_bias,
            scale2,
            fc1_bias,
            qv_bias,
            mask_row,
        ],
        1,
        jnp.bfloat16,
    )[0]
    pack_full, qkv_full = gather_parts(
        [packed, w_qkv.reshape(w_qkv.shape[0], -1)], [True, True], line, 1
    )
    qkv_full = qkv_full.reshape((-1,) + w_qkv.shape[1:])
    (
        gain_one,
        shift_one,
        bias_out,
        scale_one,
        gain_two,
        shift_two,
        bias_fc2,
        scale_two,
        bias_fc1,
    ) = [pack_full[:, i].reshape(-1) for i in range(9)]
    qv_width = qv_bias.shape[1]
    qv_full = pack_full[:, 9, : 2 * qv_width].reshape(owners, 2, qv_width)
    qv_full = qv_full.transpose(1, 0, 2).reshape(2, -1)
    mask_rows = mask_row.shape[0] // 128
    mask_part = lax.dynamic_slice_in_dim(pack_full, lax.axis_index("dp") * 2, 2, axis=0)
    full_mask = mask_part[:, 10 : 10 + mask_rows].reshape(-1)
    side = lax.axis_index("context")
    gain_one = gain_one.astype(jnp.float32)
    shift_one = shift_one.astype(jnp.float32)
    bias_out = bias_out.astype(jnp.float32)
    scale_one = scale_one.astype(jnp.float32)
    gain_two = gain_two.astype(jnp.float32)
    shift_two = shift_two.astype(jnp.float32)
    bias_fc1 = bias_fc1.astype(jnp.float32)
    bias_fc2 = bias_fc2.astype(jnp.float32)
    scale_two = scale_two.astype(jnp.float32)
    qv_float = qv_full.astype(jnp.float32)
    residual = tokens[0].astype(jnp.float32)
    row_count = residual.shape[0]
    model_width = residual.shape[1]
    local_width = qkv_full.shape[2]
    head_count = local_width // HEAD_DIM
    normed_one, inv_one = normalize(residual)
    hidden_one = (normed_one * gain_one + shift_one).astype(jnp.bfloat16)
    projected = jnp.dot(
        hidden_one,
        qkv_full.reshape(model_width, 3 * local_width),
        preferred_element_type=jnp.float32,
    ).reshape(row_count, 3, local_width)
    queries = (projected[:, 0] + qv_float[0]).astype(jnp.bfloat16)
    key_rows = projected[:, 1].astype(jnp.bfloat16)
    values = (projected[:, 2] + qv_float[1]).astype(jnp.bfloat16)
    query_heads = queries.reshape(row_count, head_count, HEAD_DIM)
    key_value = jnp.concatenate([key_rows, values], axis=1)
    far_mask = lax.dynamic_slice_in_dim(full_mask, (1 - side) * row_count, row_count, axis=0)
    out_full, fc1_full, fc2_full, other, attn_flat, log_flat = gather_parts(
        [w_out, w_fc1, w_fc2],
        [False, True, False],
        line,
        2,
        (
            queries,
            key_value,
            mask_row.astype(jnp.float32)[None],
            far_mask.astype(jnp.float32)[None],
        ),
    )
    fc1_full = fc1_full.reshape(-1, fc1_full.shape[-1])
    pair = jnp.where(
        side == 0, jnp.concatenate([key_value, other]), jnp.concatenate([other, key_value])
    )
    back_keys, back_values = pair[:, :local_width], pair[:, local_width:]
    attn_heads = attn_flat.reshape(row_count, head_count, HEAD_DIM)
    log_total = log_flat[:, :head_count].reshape(row_count, head_count, 1)
    attended = attn_heads.reshape(row_count, local_width).astype(jnp.bfloat16)
    branch = (
        tensor_sum(
            [jnp.dot(attended, out_full, preferred_element_type=jnp.float32).astype(jnp.bfloat16)], 4
        )[0].astype(jnp.float32)
        + bias_out
    )
    residual_one = residual + scale_one * branch
    normed_two, inv_two = normalize(residual_one)
    hidden_two = (normed_two * gain_two + shift_two).astype(jnp.bfloat16)
    pre_act = jnp.dot(hidden_two, fc1_full, preferred_element_type=jnp.float32) + bias_fc1
    activated, gelu_pull = jax.vjp(lambda value: jax.nn.gelu(value, approximate=False), pre_act)
    hidden = activated.astype(jnp.bfloat16)
    mlp_part = jnp.dot(hidden, fc2_full, preferred_element_type=jnp.float32).astype(jnp.bfloat16)
    grad_out = cotangent[0].astype(jnp.float32)
    grad_mlp = (grad_out * scale_two).astype(jnp.bfloat16)
    grad_bias_fc2 = jnp.sum(grad_mlp.astype(jnp.float32), axis=0)
    grad_fc2 = contract_rows(hidden, grad_mlp)
    grad_act = contract_cols(grad_mlp, fc2_full)
    grad_pre = gelu_pull(grad_act)[0].astype(jnp.bfloat16)
    grad_bias_fc1 = jnp.sum(grad_pre.astype(jnp.float32), axis=0)
    grad_fc1 = contract_rows(hidden_two, grad_pre)
    grad_part = contract_cols(grad_pre, fc1_full).astype(jnp.bfloat16)
    grad_hidden_two, mlp_sum = tensor_sum([grad_part, mlp_part], 5)
    grad_hidden_two = grad_hidden_two.astype(jnp.float32)
    mlp_out = mlp_sum.astype(jnp.float32) + bias_fc2
    block_out = (residual_one + scale_two * mlp_out).astype(jnp.bfloat16)
    grad_scale_two = jnp.sum(grad_out * mlp_out, axis=0)
    grad_gain_two = jnp.sum(grad_hidden_two * normed_two, axis=0)
    grad_shift_two = jnp.sum(grad_hidden_two, axis=0)
    grad_residual_one = grad_out + norm_backward(grad_hidden_two, normed_two, inv_two, gain_two)
    grad_scale_one = jnp.sum(grad_residual_one * branch, axis=0)
    grad_branch = (grad_residual_one * scale_one).astype(jnp.bfloat16)
    grad_bias_out = jnp.sum(grad_branch.astype(jnp.float32), axis=0)
    grad_wout = contract_rows(attended, grad_branch)
    grad_attended = contract_cols(grad_branch, out_full).astype(jnp.bfloat16)
    grad_attn_heads = grad_attended.reshape(row_count, head_count, HEAD_DIM)
    row_delta = jnp.sum(grad_attn_heads.astype(jnp.float32) * attn_heads, axis=-1, keepdims=True)
    back_mask = full_mask
    key_count = back_keys.shape[0]
    grad_query = jnp.zeros((row_count, head_count, HEAD_DIM), jnp.float32)
    key_terms = []
    value_terms = []
    for offset in range(0, key_count, 512):
        finish = min(key_count, offset + 512)
        key_block = back_keys[offset:finish].reshape(finish - offset, head_count, HEAD_DIM)
        value_block = back_values[offset:finish].reshape(finish - offset, head_count, HEAD_DIM)
        mask_block = back_mask[offset:finish][None, None, :] > 0
        scores = jnp.einsum(
            "rhe,nhe->rhn", query_heads, key_block, preferred_element_type=jnp.float32
        ) * HEAD_DIM ** (-0.5)
        attn_prob = jnp.where(mask_block, jnp.exp(scores - log_total), 0.0)
        value_terms.append(
            jnp.einsum(
                "rhn,rhe->nhe",
                attn_prob.astype(jnp.bfloat16),
                grad_attn_heads,
                preferred_element_type=jnp.float32,
            )
        )
        grad_prob = jnp.einsum(
            "rhe,nhe->rhn", grad_attn_heads, value_block, preferred_element_type=jnp.float32
        )
        grad_scores = (attn_prob * (grad_prob - row_delta)).astype(jnp.bfloat16)
        grad_query = grad_query + jnp.einsum(
            "rhn,nhe->rhe", grad_scores, key_block, preferred_element_type=jnp.float32
        ) * HEAD_DIM ** (-0.5)
        key_terms.append(
            jnp.einsum("rhn,rhe->nhe", grad_scores, query_heads, preferred_element_type=jnp.float32)
            * HEAD_DIM ** (-0.5)
        )
    key_sums = jnp.concatenate(key_terms, axis=0).reshape(key_count, local_width)
    value_sums = jnp.concatenate(value_terms, axis=0).reshape(key_count, local_width)
    sums = jnp.concatenate([key_sums, value_sums], axis=1)
    away = lax.dynamic_slice_in_dim(sums, (1 - side) * row_count, row_count, axis=0)
    home = lax.dynamic_slice_in_dim(sums, side * row_count, row_count, axis=0)
    home = home + swap(away.astype(jnp.bfloat16), 3).astype(jnp.float32)
    grad_keys, grad_values = home[:, :local_width], home[:, local_width:]
    grad_projected = jnp.stack(
        [grad_query.reshape(row_count, local_width), grad_keys, grad_values], axis=1
    ).astype(jnp.bfloat16)
    grad_float = grad_projected.astype(jnp.float32)
    grad_qv = jnp.stack(
        [jnp.sum(grad_float[:, 0], axis=0), jnp.sum(grad_float[:, 2], axis=0)], axis=0
    )
    grad_flat = grad_projected.reshape(row_count, 3 * local_width)
    grad_qkv = contract_rows(hidden_one, grad_flat)
    grad_hidden_one = tensor_sum(
        [
            contract_cols(grad_flat, qkv_full.reshape(model_width, 3 * local_width)).astype(
                jnp.bfloat16
            )
        ],
        6,
    )[0].astype(jnp.float32)
    grad_gain_one = jnp.sum(grad_hidden_one * normed_one, axis=0)
    grad_shift_one = jnp.sum(grad_hidden_one, axis=0)
    token_grad = grad_residual_one + norm_backward(grad_hidden_one, normed_one, inv_one, gain_one)
    qv_rows = grad_qv.reshape(2, owners, qv_width).transpose(1, 0, 2)
    grad_pack = pack_rows(
        [
            grad_gain_one,
            grad_shift_one,
            grad_bias_out,
            grad_scale_one,
            grad_gain_two,
            grad_shift_two,
            grad_bias_fc2,
            grad_scale_two,
            grad_bias_fc1,
            qv_rows,
        ],
        owners,
        jnp.float32,
    )
    pack_sum, qkv_sum, out_sum, fc1_sum, fc2_sum = scatter_parts(
        [
            grad_pack,
            grad_qkv.astype(jnp.bfloat16).reshape(owners, -1, 3 * local_width),
            grad_wout.astype(jnp.bfloat16),
            grad_fc1.astype(jnp.bfloat16).reshape(owners, -1, grad_fc1.shape[1]),
            grad_fc2.astype(jnp.bfloat16),
        ],
        line,
        7,
    )
    return (
        block_out[None],
        token_grad[None],
        pack_sum[0],
        pack_sum[1],
        qkv_sum.reshape(w_qkv.shape),
        pack_sum[9, : 2 * qv_width].reshape(2, qv_width),
        out_sum,
        pack_sum[2],
        pack_sum[3],
        pack_sum[4],
        pack_sum[5],
        fc1_sum,
        pack_sum[8],
        fc2_sum,
        pack_sum[6],
        pack_sum[7],
    )


def solution(mesh):
    line = mesh.shape["dp"]
    own_kernels = mesh.shape["context"] == 2 and mesh.shape["tensor"] == 4 and line == 4
    return jax.shard_map(
        functools.partial(on_device_line, line) if own_kernels else on_device,
        mesh=mesh,
        in_specs=(
            P("dp", "context", None),
            P("dp", "context"),
            P(("dp", "context")),
            P(("dp", "context")),
            P(("dp", "context"), None, "tensor"),
            P(None, ("tensor", "dp", "context")),
            P("tensor", ("dp", "context")),
            P(("dp", "context")),
            P(("dp", "context")),
            P(("dp", "context")),
            P(("dp", "context")),
            P(("dp", "context"), "tensor"),
            P(("tensor", "dp", "context")),
            P("tensor", ("dp", "context")),
            P(("dp", "context")),
            P(("dp", "context")),
            P("dp", "context", None),
        ),
        out_specs=(
            P("dp", "context", None),
            P("dp", "context", None),
            P(("dp", "context")),
            P(("dp", "context")),
            P(("dp", "context"), None, "tensor"),
            P(None, ("tensor", "dp", "context")),
            P("tensor", ("dp", "context")),
            P(("dp", "context")),
            P(("dp", "context")),
            P(("dp", "context")),
            P(("dp", "context")),
            P(("dp", "context"), "tensor"),
            P(("tensor", "dp", "context")),
            P("tensor", ("dp", "context")),
            P(("dp", "context")),
            P(("dp", "context")),
        ),
        check_vma=False,
    )
```
